32 devices in a mesh: groups: 2 (over x), wide: 16 (over z, y, core).
Axes of the slice: x: 2, y: 2, z: 4, core: 2. Of those that a mesh axis runs over, the one named last changes fastest.
Arguments:
- hidden: bfloat16 [256, 28672], P('groups', 'wide'), parts along dimension 0, may hold values from -6 to 6
- adapter_ids: int32 [256], P('groups'), parts along dimension 0, may hold values from 0 to 31, as said below
- core_slot: int32 [64], P('groups'), parts along dimension 0, may hold values from 0 to 31, as said below
- down_weight: bfloat16 [16, 3584, 6144], P('wide'), may hold values from -0.03125 to 0.03125
- rank_in: bfloat16 [28672, 512], P('wide'), may hold values from -0.03125 to 0.03125
- rank_out: bfloat16 [16, 64, 6144], P('wide'), may hold values from -0.25 to 0.25
- cores: bfloat16 [32, 512, 512], P('wide'), may hold values from -0.25 to 0.25
Outputs:
- layer_out: bfloat16 [256, 12288], P(('groups', 'wide')), parts along dimension 0
The draws below stay inside these ranges and needn't reach their ends.
There are 2 independent parts, one for each index of `groups`. The reference program is written for one: setup_inputs(seed, part) draws one part's arguments, and reference() takes and returns one part's arrays. A program takes and returns all parts, laid end to end along the dimension named above; an argument that names none is the same for every part. Nothing has to cross between parts.
Inputs may be any that keep to these rules, and one draw needn't show every extreme that they name: core_slot is a permutation of the 32 adapters. `adapter_ids`: at most 32 tokens use adapters whose core rows lie in one block of 2 rows of cores (rows j * 2 to j * 2 + 1), and some block takes exactly 32.
All inputs are finite; a program needn't handle non-finite values.
Results may differ from the reference program's by a relative error of at most 0.005.
Values may be sent and summed in bfloat16 or wider, within the bound.
A program may use at most 128 MiB of HBM per device.

```python
import jax
import jax.numpy as jnp
from jax import lax

D = 12288
FF = 28672
R = 512
FF_GROUPS = 8
ADP_DEV = 2
D_GROUPS = 2
A = 32
TOKENS = 128
OWNER_CAP = 32
N_WIDE = 16


def shared_table(key):
    return jax.random.permutation(key, A).astype(jnp.int32)


def draw_core_slot(key, part):
    return shared_table(key)


def draw_adapter_ids(key, part):
    slots = shared_table(key)
    inverse = jnp.zeros((A,), jnp.int32).at[slots].set(jnp.arange(A, dtype=jnp.int32))
    key = jax.random.fold_in(key, 7)
    first, second, third = jax.random.split(key, 3)
    order_key = jnp.arange(TOKENS, dtype=jnp.int32)
    half = TOKENS // 2
    hotcount = half // OWNER_CAP
    ranking = jnp.where(order_key < half, order_key // OWNER_CAP, hotcount + (order_key - half) % (N_WIDE - hotcount))
    scores = jax.random.randint(first, (N_WIDE,), 0, 1 << 20) * N_WIDE + jnp.arange(N_WIDE, dtype=jnp.int32)
    order = jnp.argsort(scores).astype(jnp.int32)
    owner = order[ranking]
    shuffle = jax.random.permutation(second, TOKENS)
    owner = owner[shuffle]
    local = jax.random.randint(third, (TOKENS,), 0, ADP_DEV)
    return inverse[owner * ADP_DEV + local].astype(jnp.int32)


def block_levels(rng, dims, shards, least, top_value):
    level, own = 1.0, jax.random.fold_in(rng, 6)
    for dim, parts in shards:
        heights = jnp.exp(jax.random.uniform(jax.random.fold_in(own, dim), (parts,), jnp.float32, least / len(shards), top_value / len(shards)))
        level = level * jnp.repeat(heights, dims[dim] // parts).reshape([-1 if axis == dim else 1 for axis in range(len(dims))])
    return level


def centred(stream_key, shape, scale, reach, pieces=(), kind=jnp.bfloat16):
    level = block_levels(stream_key, shape, pieces, -0.22, 0.18) if pieces else 1.0
    drawn = jax.random.normal(stream_key, shape, jnp.float32) * scale * level
    return jnp.minimum(jnp.maximum(drawn, -reach), reach).astype(kind)


def setup_inputs(seed: int = 0, part: int = 0) -> dict:
    seeds = jax.random.split(jax.random.key(seed), 8)
    own_keys = jax.random.split(jax.random.fold_in(seeds[7], part), 8)
    hidden = centred(own_keys[0], (TOKENS, FF), 1.0, 6.0, ((1, 16),))
    adapter_ids = draw_adapter_ids(jax.random.fold_in(jax.random.fold_in(seeds[7], part), 71), part)
    core_slot = draw_core_slot(jax.random.fold_in(jax.random.fold_in(seeds[7], part), 71), part)
    down_weight = centred(seeds[3], (N_WIDE, FF // FF_GROUPS, D // D_GROUPS), FF ** -0.5, 0.03125, ((0, 16),))
    rank_in = centred(seeds[4], (FF, R), FF ** -0.5, 0.03125, ((0, 16),))
    rank_out = centred(seeds[5], (N_WIDE, R // FF_GROUPS, D // D_GROUPS), R ** -0.5, 0.25, ((0, 16),))
    cores = centred(seeds[6], (A, R, R), R ** -0.5, 0.25, ((0, 16),))
    return dict(hidden=hidden, adapter_ids=adapter_ids, core_slot=core_slot, down_weight=down_weight, rank_in=rank_in, rank_out=rank_out, cores=cores)


def unblock(blocks, row_total, col_total):
    inner_rows = row_total // FF_GROUPS
    inner_cols = col_total // D_GROUPS
    shaped = blocks.reshape(FF_GROUPS, D_GROUPS, inner_rows, inner_cols)
    return jnp.transpose(shaped, (0, 2, 1, 3)).reshape(row_total, col_total)


def reference(hidden, adapter_ids, core_slot, down_weight, rank_in, rank_out, cores):
    projected = jnp.dot(hidden, rank_in, preferred_element_type=jnp.float32).astype(jnp.bfloat16)
    token_slot = core_slot[adapter_ids]

    def advance(running, position):
        product = jnp.dot(projected, cores[position], preferred_element_type=jnp.float32)
        return running + jnp.where((token_slot == position)[:, None], product, jnp.float32(0.0)), None

    initial = jnp.zeros((TOKENS, R), jnp.float32)
    lowrank, _ = lax.scan(advance, initial, jnp.arange(A, dtype=jnp.int32))
    lowrank = lowrank.astype(jnp.bfloat16)
    down_full = unblock(down_weight, FF, D)
    basis_full = unblock(rank_out, R, D)
    base = jnp.dot(hidden, down_full, preferred_element_type=jnp.float32)
    delta = jnp.dot(lowrank, basis_full, preferred_element_type=jnp.float32)
    return (base + delta).astype(jnp.bfloat16)
```

```python
import jax
import jax.numpy as jnp
from jax import lax
from jax.experimental import pallas as pl
from jax.experimental.pallas import tpu as pltpu
from jax.sharding import PartitionSpec as P

FF_GROUPS = 8
WINDOW = 3


def swapped(value, axis, distance):
    return lax.ppermute(value, axis, [(i, i ^ 1 << distance) for i in range(lax.axis_size(axis))])


def bit_value(device, bit_index):
    return device // (1 << bit_index) % 2


def general(hidden, adapter_ids, core_slot, down_weight, rank_in, rank_out, cores):
    devices = lax.axis_size("wide")
    device = lax.axis_index("wide")
    token_count = hidden.shape[0]
    rows_own = token_count // devices
    rank_size = rank_in.shape[1]
    slice_width = rank_size // devices
    adapters_all = core_slot.shape[0]
    column_groups = devices // FF_GROUPS
    low_bits = column_groups.bit_length() - 1
    block_width = down_weight.shape[2]
    partial_rank = jnp.dot(hidden, rank_in, preferred_element_type=jnp.float32)
    projected = lax.psum(partial_rank, "wide").astype(jnp.bfloat16)
    hidden_pieces = hidden
    for bit_index in range(low_bits):
        partner = swapped(hidden_pieces, "wide", bit_index)
        high_side = bit_value(device, bit_index) == 1
        hidden_pieces = jnp.where(
            high_side,
            jnp.concatenate([partner, hidden_pieces], 1),
            jnp.concatenate([hidden_pieces, partner], 1),
        )
    matches = adapter_ids[:, None] == jnp.arange(adapters_all, dtype=jnp.int32)[None, :]
    token_slot = jnp.sum(jnp.where(matches, core_slot[None, :], 0), axis=1)
    turned = jnp.transpose(cores, (1, 0, 2))
    columns = lax.all_to_all(turned, "wide", split_axis=2, concat_axis=1, tiled=True)
    products = jnp.dot(
        projected,
        columns.reshape(rank_size, adapters_all * slice_width),
        preferred_element_type=jnp.float32,
    )
    products = products.reshape(token_count, adapters_all, slice_width)
    picked = token_slot[:, None] == jnp.arange(adapters_all, dtype=jnp.int32)[None, :]
    lowrank = jnp.sum(jnp.where(picked[:, :, None], products, jnp.float32(0.0)), axis=1).astype(
        jnp.bfloat16
    )
    rank_pieces = lowrank
    for bit_index in range(low_bits):
        partner = swapped(rank_pieces, "wide", bit_index)
        high_side = bit_value(device, bit_index) == 1
        rank_pieces = jnp.where(
            high_side,
            jnp.concatenate([partner, rank_pieces], 1),
            jnp.concatenate([rank_pieces, partner], 1),
        )
    partial_value = jnp.dot(hidden_pieces, down_weight[0], preferred_element_type=jnp.float32)
    partial_value = partial_value + jnp.dot(
        rank_pieces, rank_out[0], preferred_element_type=jnp.float32
    )
    outgoing = partial_value.astype(jnp.bfloat16).reshape(devices, rows_own, block_width)
    received = lax.all_to_all(outgoing, "wide", split_axis=0, concat_axis=0, tiled=True)
    received = received.reshape(FF_GROUPS, column_groups, rows_own, block_width)
    summed = jnp.sum(received.astype(jnp.float32), axis=0)
    layer_out = jnp.transpose(summed, (1, 0, 2)).reshape(rows_own, column_groups * block_width)
    return layer_out.astype(jnp.bfloat16)


CHUNK = 768
HELD = 6
OWNER_CAP = 32
MESH = pl.DeviceIdType.MESH
F32, BF16 = jnp.float32, jnp.bfloat16


def remote(src, dst, send, recv, target):
    return pltpu.make_async_remote_copy(
        src_ref=src, dst_ref=dst, send_sem=send, recv_sem=recv, device_id={"wide": target}, device_id_type=MESH
    )


def kernel(
    ids_col, ids_row, slot_col, slot_row, hidden, weight, rank_in, rank_out, cores, out,
    hid, wbuf, rin, core_buf, vbuf, acc, pstage, precv, proj, projected, lstage, lrecv,
    ystage, yrecv, zstage, zrecv, fin, frecv,
    load_sem, w_sem, h_sem, ps_sem, pr_sem, as_sem, ar_sem, ls_sem, lr_sem,
    ys_sem, yr_sem, zs_sem, zr_sem, fs_sem, fr_sem,
):
    n = 2 * FF_GROUPS
    me = lax.axis_index("wide")
    side = lax.rem(me, 2)
    group = lax.div(me, 2)
    yy = lax.rem(group, 2)
    zz = lax.div(group, 2)
    sibling = me + 1 - 2 * side
    y_partner = me + 2 - 4 * yy
    chunks = wbuf.shape[0]
    tokens = hid.shape[0]
    units = hidden.shape[1]
    rank_rows = rank_out.shape[1]
    own_units = pl.ds(pl.multiple_of(side * units, 128), units)
    adapters = cores.shape[0]

    def w_copy(k):
        cols = pl.ds(pl.multiple_of(k * CHUNK, CHUNK), CHUNK)
        return pltpu.make_async_copy(weight.at[0, :, cols], wbuf.at[k], w_sem.at[k])

    hid_copy = pltpu.make_async_copy(hidden, hid.at[:, own_units], load_sem.at[0])
    hid_copy.start()
    rin_copy = pltpu.make_async_copy(rank_in, rin, load_sem.at[1])
    rin_copy.start()
    for k in range(WINDOW):
        w_copy(k).start()
    core_copy = pltpu.make_async_copy(cores, core_buf, load_sem.at[2])
    core_copy.start()
    half = lax.rem(group, 2)
    spare = pl.ds(pl.multiple_of((1 - half) * rank_rows, rank_rows), rank_rows)
    vbuf[spare, :] = jnp.zeros((rank_rows, vbuf.shape[1]), BF16)
    own_rank = pl.ds(pl.multiple_of(half * rank_rows, rank_rows), rank_rows)
    v_copy = pltpu.make_async_copy(rank_out.at[0], vbuf.at[own_rank, :], load_sem.at[3])
    v_copy.start()

    barrier = pltpu.get_barrier_semaphore()

    @pl.loop(1, n)
    def _(d):
        pl.semaphore_signal(barrier, inc=1, device_id={"wide": lax.rem(me + d, n)}, device_id_type=MESH)

    pl.semaphore_wait(barrier, n - 1)

    hid_copy.wait()
    h_send = remote(hid.at[:, own_units], hid.at[:, own_units], h_sem.at[0], h_sem.at[1], sibling)
    h_send.start()

    rin_copy.wait()
    partial_rank = jnp.dot(hid[:, own_units], rin[...], preferred_element_type=F32).astype(BF16)
    for c in range(FF_GROUPS):
        for s in range(2):
            pstage[2 * c + s] = partial_rank[16 * c : 16 * c + 16, 256 * s : 256 * s + 256]

    def p_copy(d):
        target = lax.rem(me + d, n)
        return remote(pstage.at[target], precv.at[me], ps_sem.at[target], pr_sem.at[me], target)

    def p_arrival(d):
        source = lax.rem(me + d, n)
        return remote(pstage.at[me], precv.at[source], ps_sem.at[source], pr_sem.at[source], source)

    @pl.loop(1, n)
    def _(d):
        p_copy(d).start()

    precv[me] = pstage[me]

    def start_next(k):
        @pl.when(k + WINDOW < chunks)
        def _():
            w_copy(k + WINDOW).start()

    def product(k):
        w_copy(k).wait()
        start_next(k)
        return jnp.dot(hid[...], wbuf[k], preferred_element_type=F32)

    def hold(first, last):
        @pl.loop(first, last)
        def _(k):
            acc[k] = product(k)

    def number(mask):
        return jnp.where(mask, 1.0, 0.0)

    all_a = slot_col.shape[0]
    lanes_a = lax.broadcasted_iota(jnp.int32, (tokens, all_a), 1)
    rows_a = lax.broadcasted_iota(jnp.int32, (all_a, tokens), 0)
    slots_c = jnp.sum(
        jnp.where(ids_col[...] == lanes_a, slot_row[...].astype(F32), 0.0), axis=1, keepdims=True
    ).astype(jnp.int32)
    slots_r = jnp.sum(
        jnp.where(ids_row[...] == rows_a, slot_col[...].astype(F32), 0.0), axis=0, keepdims=True
    ).astype(jnp.int32)
    owner_c = lax.div(slots_c, jnp.int32(adapters))
    owner_r = lax.div(slots_r, jnp.int32(adapters))
    sub = lax.broadcasted_iota(jnp.int32, (tokens, tokens), 0)
    lane = lax.broadcasted_iota(jnp.int32, (tokens, tokens), 1)
    same = owner_c == owner_r
    place_c = jnp.sum(number(same & (lane < sub)), axis=1, keepdims=True).astype(jnp.int32)
    place_r = jnp.sum(number(same & (sub < lane)), axis=0, keepdims=True).astype(jnp.int32)
    rows_p = lax.broadcasted_iota(jnp.int32, (OWNER_CAP, tokens), 0)
    mine = number((owner_r == me) & (place_r == rows_p))
    picked_slot = jnp.sum(mine * slots_r.astype(F32), axis=1, keepdims=True).astype(jnp.int32)
    lanes_s = lax.broadcasted_iota(jnp.int32, (tokens, n * OWNER_CAP), 1)

    h_send.wait()
    hold(0, 2)

    @pl.loop(1, n)
    def _(d):
        p_arrival(d).wait_recv()

    total = precv[0].astype(F32)
    for s in range(1, n):
        total += precv[s].astype(F32)
    proj[me] = total.astype(BF16)

    def a_copy(d):
        target = lax.rem(me + d, n)
        return remote(proj.at[me], proj.at[me], as_sem.at[target], ar_sem.at[me], target)

    def a_arrival(d):
        source = lax.rem(me + d, n)
        return remote(proj.at[source], proj.at[source], as_sem.at[source], ar_sem.at[source], source)

    @pl.loop(1, n)
    def _(d):
        a_copy(d).start()

    hold(2, 4)

    @pl.loop(1, n)
    def _(d):
        a_arrival(d).wait_recv()

    for c in range(FF_GROUPS):
        for s in range(2):
            projected[16 * c : 16 * c + 16, 256 * s : 256 * s + 256] = proj[2 * c + s]
    core_copy.wait()
    own = jnp.dot(mine.astype(BF16), projected[...], preferred_element_type=F32).astype(BF16)
    low = jnp.zeros(own.shape, F32)
    for a in range(adapters):
        term = jnp.dot(own, core_buf[a], preferred_element_type=F32)
        low = jnp.where(picked_slot == me * adapters + a, term, low)
    low = low.astype(BF16)
    for s in range(lstage.shape[0]):
        lstage[s] = low[:, 128 * s : 128 * s + 128]

    def l_copy(d):
        target = lax.rem(me + d, n)
        return remote(lstage.at[lax.div(target, 4)], lrecv.at[me], ls_sem.at[target], lr_sem.at[me], target)

    def l_arrival(d):
        source = lax.rem(me + d, n)
        return remote(lstage.at[0], lrecv.at[source], ls_sem.at[source], lr_sem.at[source], source)

    @pl.loop(1, n)
    def _(d):
        l_copy(d).start()

    lrecv[me] = lstage[lax.div(me, 4)]
    hold(4, HELD)

    @pl.loop(1, n)
    def _(d):
        l_arrival(d).wait_recv()

    expand = number(owner_c * OWNER_CAP + place_c == lanes_s).astype(BF16)
    arrived = lrecv[...].reshape(n * OWNER_CAP, 128)
    lowrank = jnp.dot(expand, arrived, preferred_element_type=F32).astype(BF16)
    v_copy.wait()

    def y_copy(k):
        return remote(ystage.at[k, 1 - yy], yrecv.at[k], ys_sem.at[k], yr_sem.at[k], y_partner)

    def send_y(k, value):
        cols = pl.ds(pl.multiple_of(k * CHUNK, CHUNK), CHUNK)
        value = (value + jnp.dot(lowrank, vbuf[:, cols], preferred_element_type=F32)).astype(BF16)
        for c in range(FF_GROUPS):
            ystage[k, c % 2, c // 2] = value[16 * c : 16 * c + 16]
        y_copy(k).start()

    def z_copy(k, d):
        z_to = lax.rem(zz + d, 4)
        return remote(
            zstage.at[k, z_to], zrecv.at[k, zz], zs_sem.at[k, z_to], zr_sem.at[k, zz], z_to * 4 + lax.rem(me, 4)
        )

    def z_arrival(k, d):
        z_from = lax.rem(zz + d, 4)
        return remote(
            zstage.at[k, zz], zrecv.at[k, z_from], zs_sem.at[k, z_from], zr_sem.at[k, z_from], z_from * 4 + lax.rem(me, 4)
        )

    def turn(k):
        y_copy(k).wait_recv()
        zstage[k] = (ystage[k, yy].astype(F32) + yrecv[k].astype(F32)).astype(BF16)
        for d in range(1, 4):
            z_copy(k, d).start()
        zrecv[k, zz] = zstage[k, zz]

    def f_copy(k):
        return remote(fin.at[k], frecv.at[k], fs_sem.at[k], fr_sem.at[k], sibling)

    def finish(k):
        for d in range(1, 4):
            z_arrival(k, d).wait_recv()
        fin[k] = jnp.sum(zrecv[k].astype(F32), axis=0).astype(BF16)
        f_copy(k).start()

    @pl.loop(0, HELD)
    def _(k):
        send_y(k, acc[k])

    @pl.loop(HELD, chunks)
    def _(k):
        send_y(k, product(k))
        turn(k - HELD)

    turned = chunks - HELD

    @pl.loop(turned, chunks)
    def _(k):
        turn(k)
        finish(k - turned)

    @pl.loop(chunks - turned, chunks)
    def _(k):
        finish(k)

    def rows_of(value):
        value = value.astype(F32)
        rows = value.shape[0] // 2
        return jnp.where(side == 0, value[:rows], value[rows:]).astype(out.dtype)

    @pl.loop(0, chunks)
    def _(k):
        f_copy(k).wait_recv()
        left = pl.multiple_of(side * (chunks * CHUNK) + k * CHUNK, 128)
        right = pl.multiple_of((1 - side) * (chunks * CHUNK) + k * CHUNK, 128)
        out[:, pl.ds(left, CHUNK)] = rows_of(fin[k])
        out[:, pl.ds(right, CHUNK)] = rows_of(frecv[k])

    @pl.loop(1, n)
    def _(d):
        p_copy(d).wait_send()
        a_copy(d).wait_send()
        l_copy(d).wait_send()

    @pl.loop(0, chunks)
    def _(k):
        y_copy(k).wait_send()
        f_copy(k).wait_send()
        for d in range(1, 4):
            z_copy(k, d).wait_send()


def fused(hidden, adapter_ids, core_slot, down_weight, rank_in, rank_out, cores):
    n = lax.axis_size("wide")
    tokens, units = hidden.shape
    rows, width = down_weight.shape[1:]
    chunks = width // CHUNK
    rank = rank_in.shape[1]
    adapters = core_slot.shape[0]
    anywhere = pl.BlockSpec(memory_space=pl.ANY)
    local = pl.BlockSpec(memory_space=pltpu.VMEM)
    dma = pltpu.SemaphoreType.DMA
    return pl.pallas_call(
        kernel,
        out_shape=jax.ShapeDtypeStruct((tokens // n, 2 * width), BF16),
        in_specs=[local] * 4 + [anywhere] * 5,
        out_specs=local,
        scratch_shapes=[
            pltpu.VMEM((tokens, rows), BF16),
            pltpu.VMEM((chunks, rows, CHUNK), BF16),
            pltpu.VMEM(rank_in.shape, BF16),
            pltpu.VMEM(cores.shape, BF16),
            pltpu.VMEM((128, width), BF16),
            pltpu.VMEM((HELD, tokens, CHUNK), F32),
            pltpu.VMEM((n, 16, rank // 2), BF16),
            pltpu.VMEM((n, 16, rank // 2), BF16),
            pltpu.VMEM((n, 16, rank // 2), BF16),
            pltpu.VMEM((tokens, rank), BF16),
            pltpu.VMEM((rank // 128, OWNER_CAP, 128), BF16),
            pltpu.VMEM((n, OWNER_CAP, 128), BF16),
            pltpu.VMEM((chunks, 2, 4, 16, CHUNK), BF16),
            pltpu.VMEM((chunks, 4, 16, CHUNK), BF16),
            pltpu.VMEM((chunks, 4, 16, CHUNK), BF16),
            pltpu.VMEM((chunks, 4, 16, CHUNK), BF16),
            pltpu.VMEM((chunks, 16, CHUNK), BF16),
            pltpu.VMEM((chunks, 16, CHUNK), BF16),
            dma((4,)), dma((chunks,)), dma((2,)),
            dma((n,)), dma((n,)), dma((n,)), dma((n,)), dma((n,)), dma((n,)),
            dma((chunks,)), dma((chunks,)), dma((chunks, 4)), dma((chunks, 4)),
            dma((chunks,)), dma((chunks,)),
        ],
        compiler_params=pltpu.CompilerParams(
            collective_id=0, has_side_effects=True, vmem_limit_bytes=60 * 1024 * 1024
        ),
        cost_estimate=pl.CostEstimate(
            flops=2 * tokens * rows * width, bytes_accessed=2 * rows * width, transcendentals=0
        ),
    )(
        adapter_ids.reshape(tokens, 1), adapter_ids.reshape(1, tokens),
        core_slot.reshape(adapters, 1), core_slot.reshape(1, adapters),
        hidden, down_weight, rank_in, rank_out, cores,
    )


def fits(devices, args):
    hidden, down_weight, rank_in = args[0], args[3], args[4]
    return (
        devices == 2 * FF_GROUPS
        and hidden.shape[0] == 16 * FF_GROUPS
        and rank_in.shape[1] == 64 * FF_GROUPS
        and down_weight.shape[2] % CHUNK == 0
        and down_weight.shape[2] // CHUNK >= HELD
    )


def shards(*args):
    return fused(*args) if fits(lax.axis_size("wide"), args) else general(*args)


def solution(mesh):
    return jax.shard_map(
        shards,
        mesh=mesh,
        in_specs=(
            P("groups", "wide"),
            P("groups"),
            P("groups"),
            P("wide", None, None),
            P("wide", None),
            P("wide", None, None),
            P("wide", None, None),
        ),
        out_specs=P(("groups", "wide"), None),
        check_vma=False,
    )
```

```python
import jax
import jax.numpy as jnp
from jax import lax
from jax.experimental import pallas as pl
from jax.experimental.pallas import tpu as pltpu
from jax.sharding import PartitionSpec as P

FF_GROUPS = 8
WINDOW = 4


def swapped(value, axis, distance):
    return lax.ppermute(value, axis, [(i, i ^ 1 << distance) for i in range(lax.axis_size(axis))])


def bit_value(device, bit_index):
    return device // (1 << bit_index) % 2


def general(hidden, adapter_ids, core_slot, down_weight, rank_in, rank_out, cores):
    devices = lax.axis_size("wide")
    device = lax.axis_index("wide")
    token_count = hidden.shape[0]
    rows_own = token_count // devices
    rank_size = rank_in.shape[1]
    slice_width = rank_size // devices
    adapters_all = core_slot.shape[0]
    column_groups = devices // FF_GROUPS
    low_bits = column_groups.bit_length() - 1
    block_width = down_weight.shape[2]
    partial_rank = jnp.dot(hidden, rank_in, preferred_element_type=jnp.float32)
    projected = lax.psum(partial_rank, "wide").astype(jnp.bfloat16)
    hidden_pieces = hidden
    for bit_index in range(low_bits):
        partner = swapped(hidden_pieces, "wide", bit_index)
        high_side = bit_value(device, bit_index) == 1
        hidden_pieces = jnp.where(
            high_side,
            jnp.concatenate([partner, hidden_pieces], 1),
            jnp.concatenate([hidden_pieces, partner], 1),
        )
    matches = adapter_ids[:, None] == jnp.arange(adapters_all, dtype=jnp.int32)[None, :]
    token_slot = jnp.sum(jnp.where(matches, core_slot[None, :], 0), axis=1)
    turned = jnp.transpose(cores, (1, 0, 2))
    columns = lax.all_to_all(turned, "wide", split_axis=2, concat_axis=1, tiled=True)
    products = jnp.dot(
        projected,
        columns.reshape(rank_size, adapters_all * slice_width),
        preferred_element_type=jnp.float32,
    )
    products = products.reshape(token_count, adapters_all, slice_width)
    picked = token_slot[:, None] == jnp.arange(adapters_all, dtype=jnp.int32)[None, :]
    lowrank = jnp.sum(jnp.where(picked[:, :, None], products, jnp.float32(0.0)), axis=1).astype(
        jnp.bfloat16
    )
    rank_pieces = lowrank
    for bit_index in range(low_bits):
        partner = swapped(rank_pieces, "wide", bit_index)
        high_side = bit_value(device, bit_index) == 1
        rank_pieces = jnp.where(
            high_side,
            jnp.concatenate([partner, rank_pieces], 1),
            jnp.concatenate([rank_pieces, partner], 1),
        )
    partial_value = jnp.dot(hidden_pieces, down_weight[0], preferred_element_type=jnp.float32)
    partial_value = partial_value + jnp.dot(
        rank_pieces, rank_out[0], preferred_element_type=jnp.float32
    )
    outgoing = partial_value.astype(jnp.bfloat16).reshape(devices, rows_own, block_width)
    received = lax.all_to_all(outgoing, "wide", split_axis=0, concat_axis=0, tiled=True)
    received = received.reshape(FF_GROUPS, column_groups, rows_own, block_width)
    summed = jnp.sum(received.astype(jnp.float32), axis=0)
    layer_out = jnp.transpose(summed, (1, 0, 2)).reshape(rows_own, column_groups * block_width)
    return layer_out.astype(jnp.bfloat16)


CHUNK = 768
HELD = 6
EARLY, SECOND = 2, 4
OWNER_CAP = 32
MESH = pl.DeviceIdType.MESH
F32, BF16 = jnp.float32, jnp.bfloat16


def remote(src, dst, send, recv, target):
    return pltpu.make_async_remote_copy(
        src_ref=src, dst_ref=dst, send_sem=send, recv_sem=recv, device_id={"wide": target}, device_id_type=MESH
    )


def kernel(
    ids_row, slot_row, hidden, weight, rank_in, rank_out, cores, out,
    hid, wbuf, rin, core_buf, vbuf, acc, pstage, precv, proj, projected, lstage, lrecv,
    ystage, yown, yrecv, zstage, zrecv, fin, frecv,
    load_sem, w_sem, h_sem, ps_sem, pr_sem, as_sem, ar_sem, ls_sem, lr_sem,
    ys_sem, yr_sem, zs_sem, zr_sem, fs_sem, fr_sem, vs_sem, vr_sem,
):
    n = 2 * FF_GROUPS
    me = lax.axis_index("wide")
    side = lax.rem(me, 2)
    group = lax.div(me, 2)
    yy = lax.rem(group, 2)
    zz = lax.div(group, 2)
    sibling = me + 1 - 2 * side
    y_partner = me + 2 - 4 * yy
    chunks = wbuf.shape[0]
    tokens = hid.shape[0]
    units = hidden.shape[1]
    rank_rows = rank_out.shape[1]
    own_units = pl.ds(pl.multiple_of(side * units, 128), units)
    adapters = cores.shape[0]

    def w_copy(k):
        cols = pl.ds(pl.multiple_of(k * CHUNK, CHUNK), CHUNK)
        return pltpu.make_async_copy(weight.at[0, :, cols], wbuf.at[k], w_sem.at[k])

    hid_copy = pltpu.make_async_copy(hidden, hid.at[:, own_units], load_sem.at[0])
    hid_copy.start()
    rin_copy = pltpu.make_async_copy(rank_in, rin, load_sem.at[1])
    rin_copy.start()
    half = lax.rem(group, 2)
    spare = pl.ds(pl.multiple_of((1 - half) * rank_rows, rank_rows), rank_rows)
    vbuf[spare, EARLY * CHUNK :] = jnp.zeros((rank_rows, vbuf.shape[1] - EARLY * CHUNK), BF16)
    own_rank = pl.ds(pl.multiple_of(half * rank_rows, rank_rows), rank_rows)
    v_copy = pltpu.make_async_copy(rank_out.at[0], vbuf.at[own_rank, :], load_sem.at[3])
    v_copy.start()
    for k in range(WINDOW):
        w_copy(k).start(priority=1)
    core_copy = pltpu.make_async_copy(cores, core_buf, load_sem.at[2])
    core_copy.start()

    barrier = pltpu.get_barrier_semaphore()

    @pl.loop(1, n)
    def _(d):
        pl.semaphore_signal(barrier, inc=1, device_id={"wide": lax.rem(me + d, n)}, device_id_type=MESH)


    hid_copy.wait()
    rin_copy.wait()
    partial_rank = jnp.dot(hid[:, own_units], rin[...], preferred_element_type=F32).astype(BF16)
    for c in range(FF_GROUPS):
        for s in range(2):
            pstage[2 * c + s] = partial_rank[16 * c : 16 * c + 16, 256 * s : 256 * s + 256]

    def number(mask):
        return jnp.where(mask, 1.0, 0.0)

    def column(row):
        size = row.shape[1]
        eye = lax.broadcasted_iota(jnp.int32, (size, size), 0) == lax.broadcasted_iota(jnp.int32, (size, size), 1)
        return jnp.sum(jnp.where(eye, row.astype(F32), 0.0), axis=1, keepdims=True).astype(jnp.int32)

    all_a = slot_row.shape[1]
    ids_col, slot_col = column(ids_row[...]), column(slot_row[...])
    lanes_a = lax.broadcasted_iota(jnp.int32, (tokens, all_a), 1)
    rows_a = lax.broadcasted_iota(jnp.int32, (all_a, tokens), 0)
    slots_c = jnp.sum(
        jnp.where(ids_col == lanes_a, slot_row[...].astype(F32), 0.0), axis=1, keepdims=True
    ).astype(jnp.int32)
    slots_r = jnp.sum(
        jnp.where(ids_row[...] == rows_a, slot_col.astype(F32), 0.0), axis=0, keepdims=True
    ).astype(jnp.int32)
    owner_c = lax.div(slots_c, jnp.int32(adapters))
    owner_r = lax.div(slots_r, jnp.int32(adapters))
    sub = lax.broadcasted_iota(jnp.int32, (tokens, tokens), 0)
    lane = lax.broadcasted_iota(jnp.int32, (tokens, tokens), 1)
    same = owner_c == owner_r
    place_c = jnp.sum(number(same & (lane < sub)), axis=1, keepdims=True).astype(jnp.int32)
    place_r = jnp.sum(number(same & (sub < lane)), axis=0, keepdims=True).astype(jnp.int32)
    rows_p = lax.broadcasted_iota(jnp.int32, (OWNER_CAP, tokens), 0)
    mine = number((owner_r == me) & (place_r == rows_p))
    picked_slot = jnp.sum(mine * slots_r.astype(F32), axis=1, keepdims=True).astype(jnp.int32)
    lanes_s = lax.broadcasted_iota(jnp.int32, (tokens, n * OWNER_CAP), 1)

    pl.semaphore_wait(barrier, n - 1)
    h_send = remote(hid.at[:, own_units], hid.at[:, own_units], h_sem.at[0], h_sem.at[1], sibling)
    h_send.start()

    def p_copy(d):
        target = lax.rem(me + d, n)
        return remote(pstage.at[target], precv.at[me], ps_sem.at[target], pr_sem.at[me], target)

    def p_arrival(d):
        source = lax.rem(me + d, n)
        return remote(pstage.at[me], precv.at[source], ps_sem.at[source], pr_sem.at[source], source)

    @pl.loop(1, n)
    def _(d):
        p_copy(d).start()

    precv[me] = pstage[me]
    v_copy.wait()

    def v_move(k, rows):
        part = vbuf.at[rows, pl.ds(pl.multiple_of(k * CHUNK, CHUNK), CHUNK)]
        return remote(part, part, vs_sem.at[k], vr_sem.at[k], y_partner)

    for k in range(EARLY):
        v_move(k, own_rank).start()

    def start_next(k):
        @pl.when(k + WINDOW < chunks)
        def _():
            w_copy(k + WINDOW).start(priority=1)

    def product(k):
        w_copy(k).wait()
        start_next(k)
        return jnp.dot(hid[...], wbuf[k], preferred_element_type=F32)

    def hold(first, last):
        @pl.loop(first, last)
        def _(k):
            acc[k] = product(k)

    h_send.wait()
    def y_copy(k):
        return remote(ystage.at[k], yrecv.at[k], ys_sem.at[k], yr_sem.at[k], y_partner)

    def send_y(k, value):
        for c in range(0, FF_GROUPS, 2):
            even, odd = value[16 * c : 16 * c + 16], value[16 * c + 16 : 16 * c + 32]
            ystage[k, c // 2] = jnp.where(yy == 0, odd, even).astype(BF16)
            yown[k, c // 2] = jnp.where(yy == 0, even, odd)
        y_copy(k).start()

    @pl.loop(0, EARLY)
    def _(k):
        send_y(k, product(k))


    @pl.loop(1, n)
    def _(d):
        p_arrival(d).wait_recv()

    total = precv[0].astype(F32)
    for s in range(1, n):
        total += precv[s].astype(F32)
    proj[me] = total.astype(BF16)

    def a_copy(d):
        target = lax.rem(me + d, n)
        return remote(proj.at[me], proj.at[me], as_sem.at[target], ar_sem.at[me], target)

    def a_arrival(d):
        source = lax.rem(me + d, n)
        return remote(proj.at[source], proj.at[source], as_sem.at[source], ar_sem.at[source], source)

    @pl.loop(1, n)
    def _(d):
        a_copy(d).start()

    hold(EARLY, SECOND)

    @pl.loop(1, n)
    def _(d):
        a_arrival(d).wait_recv()

    for c in range(FF_GROUPS):
        for s in range(2):
            projected[16 * c : 16 * c + 16, 256 * s : 256 * s + 256] = proj[2 * c + s]
    core_copy.wait()
    own = jnp.dot(mine.astype(BF16), projected[...], preferred_element_type=F32).astype(BF16)
    low = jnp.zeros(own.shape, F32)
    for a in range(adapters):
        term = jnp.dot(own, core_buf[a], preferred_element_type=F32)
        low = jnp.where(picked_slot == me * adapters + a, term, low)
    low = low.astype(BF16)
    for s in range(lstage.shape[0]):
        lstage[s] = low[:, 128 * s : 128 * s + 128]

    def l_copy(d):
        target = lax.rem(me + d, n)
        return remote(lstage.at[lax.div(target, 4)], lrecv.at[me], ls_sem.at[target], lr_sem.at[me], target)

    def l_arrival(d):
        source = lax.rem(me + d, n)
        return remote(lstage.at[0], lrecv.at[source], ls_sem.at[source], lr_sem.at[source], source)

    @pl.loop(1, n)
    def _(d):
        l_copy(d).start()

    lrecv[me] = lstage[lax.div(me, 4)]
    hold(SECOND, HELD)

    @pl.loop(1, n)
    def _(d):
        l_arrival(d).wait_recv()

    expand = number(owner_c * OWNER_CAP + place_c == lanes_s).astype(BF16)
    arrived = lrecv[...].reshape(n * OWNER_CAP, 128)
    lowrank = jnp.dot(expand, arrived, preferred_element_type=F32)
    kept = []
    for c in range(0, FF_GROUPS, 2):
        kept.append(jnp.where(yy == 0, lowrank[16 * c : 16 * c + 16], lowrank[16 * c + 16 : 16 * c + 32]))
    kept = jnp.concatenate(kept, 0).astype(BF16)
    lowrank = lowrank.astype(BF16)

    def adapter_term(rows, k):
        cols = pl.ds(pl.multiple_of(k * CHUNK, CHUNK), CHUNK)
        return jnp.dot(rows, vbuf[:, cols], preferred_element_type=F32)


    def z_copy(k, d):
        z_to = lax.rem(zz + d, 4)
        return remote(
            zstage.at[k, z_to], zrecv.at[k, zz], zs_sem.at[k, z_to], zr_sem.at[k, zz], z_to * 4 + lax.rem(me, 4)
        )

    def z_arrival(k, d):
        z_from = lax.rem(zz + d, 4)
        return remote(
            zstage.at[k, zz], zrecv.at[k, z_from], zs_sem.at[k, z_from], zr_sem.at[k, z_from], z_from * 4 + lax.rem(me, 4)
        )

    def turn(k, early):
        y_copy(k).wait_recv()
        pair = yown[k] + yrecv[k].astype(F32)
        if early:
            v_move(k, spare).wait_recv()
            pair += adapter_term(kept, k).reshape(pair.shape)
        zstage[k] = pair.astype(BF16)
        yown[k] = pair
        for d in range(1, 4):
            z_copy(k, d).start()

    def f_copy(k):
        return remote(fin.at[k], frecv.at[k], fs_sem.at[k], fr_sem.at[k], sibling)

    def finish(k):
        for d in range(1, 4):
            z_arrival(k, d).wait_recv()
        value = yown[k, zz]
        for d in range(1, 4):
            value += zrecv[k, lax.rem(zz + d, 4)].astype(F32)
        fin[k] = value.astype(BF16)
        f_copy(k).start()

    @pl.loop(EARLY, HELD)
    def _(k):
        send_y(k, acc[k] + adapter_term(lowrank, k))

    @pl.loop(0, EARLY)
    def _(k):
        turn(k, True)

    @pl.loop(HELD, chunks)
    def _(k):
        send_y(k, product(k) + adapter_term(lowrank, k))

    @pl.loop(EARLY, chunks)
    def _(k):
        turn(k, False)
        finish(k - EARLY)

    @pl.loop(chunks - EARLY, chunks)
    def _(k):
        finish(k)

    def rows_of(value):
        value = value.astype(F32)
        rows = value.shape[0] // 2
        return jnp.where(side == 0, value[:rows], value[rows:]).astype(out.dtype)

    @pl.loop(0, chunks)
    def _(k):
        f_copy(k).wait_recv()
        left = pl.multiple_of(side * (chunks * CHUNK) + k * CHUNK, 128)
        right = pl.multiple_of((1 - side) * (chunks * CHUNK) + k * CHUNK, 128)
        out[:, pl.ds(left, CHUNK)] = rows_of(fin[k])
        out[:, pl.ds(right, CHUNK)] = rows_of(frecv[k])

    @pl.loop(1, n)
    def _(d):
        p_copy(d).wait_send()
        a_copy(d).wait_send()
        l_copy(d).wait_send()

    for k in range(EARLY):
        v_move(k, own_rank).wait_send()

    @pl.loop(0, chunks)
    def _(k):
        y_copy(k).wait_send()
        f_copy(k).wait_send()
        for d in range(1, 4):
            z_copy(k, d).wait_send()


def fused(hidden, adapter_ids, core_slot, down_weight, rank_in, rank_out, cores):
    n = lax.axis_size("wide")
    tokens, units = hidden.shape
    rows, width = down_weight.shape[1:]
    chunks = width // CHUNK
    rank = rank_in.shape[1]
    adapters = core_slot.shape[0]
    anywhere = pl.BlockSpec(memory_space=pl.ANY)
    local = pl.BlockSpec(memory_space=pltpu.VMEM)
    dma = pltpu.SemaphoreType.DMA
    return pl.pallas_call(
        kernel,
        out_shape=jax.ShapeDtypeStruct((tokens // n, 2 * width), BF16),
        in_specs=[local] * 2 + [anywhere] * 5,
        out_specs=local,
        scratch_shapes=[
            pltpu.VMEM((tokens, rows), BF16),
            pltpu.VMEM((chunks, rows, CHUNK), BF16),
            pltpu.VMEM(rank_in.shape, BF16),
            pltpu.VMEM(cores.shape, BF16),
            pltpu.VMEM((128, width), BF16),
            pltpu.VMEM((HELD, tokens, CHUNK), F32),
            pltpu.VMEM((n, 16, rank // 2), BF16),
            pltpu.VMEM((n, 16, rank // 2), BF16),
            pltpu.VMEM((n, 16, rank // 2), BF16),
            pltpu.VMEM((tokens, rank), BF16),
            pltpu.VMEM((rank // 128, OWNER_CAP, 128), BF16),
            pltpu.VMEM((n, OWNER_CAP, 128), BF16),
            pltpu.VMEM((chunks, 4, 16, CHUNK), BF16),
            pltpu.VMEM((chunks, 4, 16, CHUNK), F32),
            pltpu.VMEM((chunks, 4, 16, CHUNK), BF16),
            pltpu.VMEM((chunks, 4, 16, CHUNK), BF16),
            pltpu.VMEM((chunks, 4, 16, CHUNK), BF16),
            pltpu.VMEM((chunks, 16, CHUNK), BF16),
            pltpu.VMEM((chunks, 16, CHUNK), BF16),
            dma((4,)), dma((chunks,)), dma((2,)),
            dma((n,)), dma((n,)), dma((n,)), dma((n,)), dma((n,)), dma((n,)),
            dma((chunks,)), dma((chunks,)), dma((chunks, 4)), dma((chunks, 4)),
            dma((chunks,)), dma((chunks,)), dma((EARLY,)), dma((EARLY,)),
        ],
        compiler_params=pltpu.CompilerParams(
            collective_id=0, has_side_effects=True, vmem_limit_bytes=60 * 1024 * 1024
        ),
        cost_estimate=pl.CostEstimate(
            flops=2 * tokens * rows * width, bytes_accessed=2 * rows * width, transcendentals=0
        ),
    )(
        adapter_ids.reshape(1, tokens), core_slot.reshape(1, adapters),
        hidden, down_weight, rank_in, rank_out, cores,
    )


def fits(devices, args):
    hidden, down_weight, rank_in = args[0], args[3], args[4]
    return (
        devices == 2 * FF_GROUPS
        and hidden.shape[0] == 16 * FF_GROUPS
        and rank_in.shape[1] == 64 * FF_GROUPS
        and down_weight.shape[2] % CHUNK == 0
        and down_weight.shape[2] // CHUNK >= HELD
    )


def shards(*args):
    return fused(*args) if fits(lax.axis_size("wide"), args) else general(*args)


def solution(mesh):
    return jax.shard_map(
        shards,
        mesh=mesh,
        in_specs=(
            P("groups", "wide"),
            P("groups"),
            P("groups"),
            P("wide", None, None),
            P("wide", None),
            P("wide", None, None),
            P("wide", None, None),
        ),
        out_specs=P(("groups", "wide"), None),
        check_vma=False,
    )
```

```python
import jax
import jax.numpy as jnp
from jax import lax
from jax.experimental import pallas as pl
from jax.experimental.pallas import tpu as pltpu
from jax.sharding import PartitionSpec as P

FF_GROUPS = 8
WINDOW = 3


def swapped(value, axis, distance):
    return lax.ppermute(value, axis, [(i, i ^ 1 << distance) for i in range(lax.axis_size(axis))])


def bit_value(device, bit_index):
    return device // (1 << bit_index) % 2


def general(hidden, adapter_ids, core_slot, down_weight, rank_in, rank_out, cores):
    devices = lax.axis_size("wide")
    device = lax.axis_index("wide")
    token_count = hidden.shape[0]
    rows_own = token_count // devices
    rank_size = rank_in.shape[1]
    slice_width = rank_size // devices
    adapters_all = core_slot.shape[0]
    column_groups = devices // FF_GROUPS
    low_bits = column_groups.bit_length() - 1
    block_width = down_weight.shape[2]
    partial_rank = jnp.dot(hidden, rank_in, preferred_element_type=jnp.float32)
    projected = lax.psum(partial_rank, "wide").astype(jnp.bfloat16)
    hidden_pieces = hidden
    for bit_index in range(low_bits):
        partner = swapped(hidden_pieces, "wide", bit_index)
        high_side = bit_value(device, bit_index) == 1
        hidden_pieces = jnp.where(
            high_side,
            jnp.concatenate([partner, hidden_pieces], 1),
            jnp.concatenate([hidden_pieces, partner], 1),
        )
    matches = adapter_ids[:, None] == jnp.arange(adapters_all, dtype=jnp.int32)[None, :]
    token_slot = jnp.sum(jnp.where(matches, core_slot[None, :], 0), axis=1)
    turned = jnp.transpose(cores, (1, 0, 2))
    columns = lax.all_to_all(turned, "wide", split_axis=2, concat_axis=1, tiled=True)
    products = jnp.dot(
        projected,
        columns.reshape(rank_size, adapters_all * slice_width),
        preferred_element_type=jnp.float32,
    )
    products = products.reshape(token_count, adapters_all, slice_width)
    picked = token_slot[:, None] == jnp.arange(adapters_all, dtype=jnp.int32)[None, :]
    lowrank = jnp.sum(jnp.where(picked[:, :, None], products, jnp.float32(0.0)), axis=1).astype(
        jnp.bfloat16
    )
    rank_pieces = lowrank
    for bit_index in range(low_bits):
        partner = swapped(rank_pieces, "wide", bit_index)
        high_side = bit_value(device, bit_index) == 1
        rank_pieces = jnp.where(
            high_side,
            jnp.concatenate([partner, rank_pieces], 1),
            jnp.concatenate([rank_pieces, partner], 1),
        )
    partial_value = jnp.dot(hidden_pieces, down_weight[0], preferred_element_type=jnp.float32)
    partial_value = partial_value + jnp.dot(
        rank_pieces, rank_out[0], preferred_element_type=jnp.float32
    )
    outgoing = partial_value.astype(jnp.bfloat16).reshape(devices, rows_own, block_width)
    received = lax.all_to_all(outgoing, "wide", split_axis=0, concat_axis=0, tiled=True)
    received = received.reshape(FF_GROUPS, column_groups, rows_own, block_width)
    summed = jnp.sum(received.astype(jnp.float32), axis=0)
    layer_out = jnp.transpose(summed, (1, 0, 2)).reshape(rows_own, column_groups * block_width)
    return layer_out.astype(jnp.bfloat16)


CHUNK = 1024
HELD = 5
EARLY, SECOND = 1, 3
OWNER_CAP = 32
MESH = pl.DeviceIdType.MESH
F32, BF16 = jnp.float32, jnp.bfloat16


def remote(src, dst, send, recv, target):
    return pltpu.make_async_remote_copy(
        src_ref=src, dst_ref=dst, send_sem=send, recv_sem=recv, device_id={"wide": target}, device_id_type=MESH
    )


def kernel(
    ids_row, slot_row, hidden, weight, rank_in, rank_out, cores, out,
    hid, wbuf, rin, core_buf, vbuf, acc, pstage, precv, proj, projected, lstage, lrecv,
    ystage, yown, yrecv, zstage, zrecv, fin, frecv,
    load_sem, w_sem, h_sem, ps_sem, pr_sem, as_sem, ar_sem, ls_sem, lr_sem,
    ys_sem, yr_sem, zs_sem, zr_sem, fs_sem, fr_sem, vs_sem, vr_sem,
):
    n = 2 * FF_GROUPS
    me = lax.axis_index("wide")
    side = lax.rem(me, 2)
    group = lax.div(me, 2)
    yy = lax.rem(group, 2)
    zz = lax.div(group, 2)
    sibling = me + 1 - 2 * side
    y_partner = me + 2 - 4 * yy
    chunks = wbuf.shape[0]
    tokens = hid.shape[0]
    units = hidden.shape[1]
    rank_rows = rank_out.shape[1]
    own_units = pl.ds(pl.multiple_of(side * units, 128), units)
    adapters = cores.shape[0]

    def w_copy(k):
        cols = pl.ds(pl.multiple_of(k * CHUNK, CHUNK), CHUNK)
        return pltpu.make_async_copy(weight.at[0, :, cols], wbuf.at[k], w_sem.at[k])

    hid_copy = pltpu.make_async_copy(hidden, hid.at[:, own_units], load_sem.at[0])
    hid_copy.start()
    rin_copy = pltpu.make_async_copy(rank_in, rin, load_sem.at[1])
    rin_copy.start()
    half = lax.rem(group, 2)
    spare = pl.ds(pl.multiple_of((1 - half) * rank_rows, rank_rows), rank_rows)
    vbuf[spare, EARLY * CHUNK :] = jnp.zeros((rank_rows, vbuf.shape[1] - EARLY * CHUNK), BF16)
    own_rank = pl.ds(pl.multiple_of(half * rank_rows, rank_rows), rank_rows)
    v_copy = pltpu.make_async_copy(rank_out.at[0], vbuf.at[own_rank, :], load_sem.at[3])
    v_copy.start()
    for k in range(WINDOW):
        w_copy(k).start(priority=1)
    core_copy = pltpu.make_async_copy(cores, core_buf, load_sem.at[2])
    core_copy.start()

    barrier = pltpu.get_barrier_semaphore()

    @pl.loop(1, n)
    def _(d):
        pl.semaphore_signal(barrier, inc=1, device_id={"wide": lax.rem(me + d, n)}, device_id_type=MESH)


    hid_copy.wait()
    rin_copy.wait()
    partial_rank = jnp.dot(hid[:, own_units], rin[...], preferred_element_type=F32).astype(BF16)
    for c in range(FF_GROUPS):
        for s in range(2):
            pstage[2 * c + s] = partial_rank[16 * c : 16 * c + 16, 256 * s : 256 * s + 256]

    def number(mask):
        return jnp.where(mask, 1.0, 0.0)

    def column(row):
        size = row.shape[1]
        eye = lax.broadcasted_iota(jnp.int32, (size, size), 0) == lax.broadcasted_iota(jnp.int32, (size, size), 1)
        return jnp.sum(jnp.where(eye, row.astype(F32), 0.0), axis=1, keepdims=True).astype(jnp.int32)

    all_a = slot_row.shape[1]
    ids_col, slot_col = column(ids_row[...]), column(slot_row[...])
    lanes_a = lax.broadcasted_iota(jnp.int32, (tokens, all_a), 1)
    rows_a = lax.broadcasted_iota(jnp.int32, (all_a, tokens), 0)
    slots_c = jnp.sum(
        jnp.where(ids_col == lanes_a, slot_row[...].astype(F32), 0.0), axis=1, keepdims=True
    ).astype(jnp.int32)
    slots_r = jnp.sum(
        jnp.where(ids_row[...] == rows_a, slot_col.astype(F32), 0.0), axis=0, keepdims=True
    ).astype(jnp.int32)
    owner_c = lax.div(slots_c, jnp.int32(adapters))
    owner_r = lax.div(slots_r, jnp.int32(adapters))
    sub = lax.broadcasted_iota(jnp.int32, (tokens, tokens), 0)
    lane = lax.broadcasted_iota(jnp.int32, (tokens, tokens), 1)
    same = owner_c == owner_r
    place_c = jnp.sum(number(same & (lane < sub)), axis=1, keepdims=True).astype(jnp.int32)
    place_r = jnp.sum(number(same & (sub < lane)), axis=0, keepdims=True).astype(jnp.int32)
    rows_p = lax.broadcasted_iota(jnp.int32, (OWNER_CAP, tokens), 0)
    mine = number((owner_r == me) & (place_r == rows_p))
    picked_slot = jnp.sum(mine * slots_r.astype(F32), axis=1, keepdims=True).astype(jnp.int32)
    lanes_s = lax.broadcasted_iota(jnp.int32, (tokens, n * OWNER_CAP), 1)

    pl.semaphore_wait(barrier, n - 1)
    h_send = remote(hid.at[:, own_units], hid.at[:, own_units], h_sem.at[0], h_sem.at[1], sibling)
    h_send.start()

    def p_copy(d):
        target = lax.rem(me + d, n)
        return remote(pstage.at[target], precv.at[me], ps_sem.at[target], pr_sem.at[me], target)

    def p_arrival(d):
        source = lax.rem(me + d, n)
        return remote(pstage.at[me], precv.at[source], ps_sem.at[source], pr_sem.at[source], source)

    @pl.loop(1, n)
    def _(d):
        p_copy(d).start()

    precv[me] = pstage[me]
    v_copy.wait()

    def v_move(k, rows):
        part = vbuf.at[rows, pl.ds(pl.multiple_of(k * CHUNK, CHUNK), CHUNK)]
        return remote(part, part, vs_sem.at[k], vr_sem.at[k], y_partner)

    for k in range(EARLY):
        v_move(k, own_rank).start()

    def start_next(k):
        @pl.when(k + WINDOW < chunks)
        def _():
            w_copy(k + WINDOW).start(priority=1)

    def product(k):
        w_copy(k).wait()
        start_next(k)
        return jnp.dot(hid[...], wbuf[k], preferred_element_type=F32)

    def hold(first, last):
        @pl.loop(first, last)
        def _(k):
            acc[k] = product(k)

    h_send.wait()
    def y_copy(k):
        return remote(ystage.at[k], yrecv.at[k], ys_sem.at[k], yr_sem.at[k], y_partner)

    def send_y(k, value):
        for c in range(0, FF_GROUPS, 2):
            even, odd = value[16 * c : 16 * c + 16], value[16 * c + 16 : 16 * c + 32]
            ystage[k, c // 2] = jnp.where(yy == 0, odd, even).astype(BF16)
            yown[k, c // 2] = jnp.where(yy == 0, even, odd)
        y_copy(k).start()

    @pl.loop(0, EARLY)
    def _(k):
        send_y(k, product(k))


    @pl.loop(1, n)
    def _(d):
        p_arrival(d).wait_recv()

    total = precv[0].astype(F32)
    for s in range(1, n):
        total += precv[s].astype(F32)
    proj[me] = total.astype(BF16)

    def a_copy(d):
        target = lax.rem(me + d, n)
        return remote(proj.at[me], proj.at[me], as_sem.at[target], ar_sem.at[me], target)

    def a_arrival(d):
        source = lax.rem(me + d, n)
        return remote(proj.at[source], proj.at[source], as_sem.at[source], ar_sem.at[source], source)

    @pl.loop(1, n)
    def _(d):
        a_copy(d).start()

    hold(EARLY, SECOND)

    @pl.loop(1, n)
    def _(d):
        a_arrival(d).wait_recv()

    for c in range(FF_GROUPS):
        for s in range(2):
            projected[16 * c : 16 * c + 16, 256 * s : 256 * s + 256] = proj[2 * c + s]
    core_copy.wait()
    own = jnp.dot(mine.astype(BF16), projected[...], preferred_element_type=F32).astype(BF16)
    low = jnp.zeros(own.shape, F32)
    for a in range(adapters):
        term = jnp.dot(own, core_buf[a], preferred_element_type=F32)
        low = jnp.where(picked_slot == me * adapters + a, term, low)
    low = low.astype(BF16)
    for s in range(lstage.shape[0]):
        lstage[s] = low[:, 128 * s : 128 * s + 128]

    def l_copy(d):
        target = lax.rem(me + d, n)
        return remote(lstage.at[lax.div(target, 4)], lrecv.at[me], ls_sem.at[target], lr_sem.at[me], target)

    def l_arrival(d):
        source = lax.rem(me + d, n)
        return remote(lstage.at[0], lrecv.at[source], ls_sem.at[source], lr_sem.at[source], source)

    @pl.loop(1, n)
    def _(d):
        l_copy(d).start()

    lrecv[me] = lstage[lax.div(me, 4)]
    hold(SECOND, HELD)

    @pl.loop(1, n)
    def _(d):
        l_arrival(d).wait_recv()

    expand = number(owner_c * OWNER_CAP + place_c == lanes_s).astype(BF16)
    arrived = lrecv[...].reshape(n * OWNER_CAP, 128)
    lowrank = jnp.dot(expand, arrived, preferred_element_type=F32)
    kept = []
    for c in range(0, FF_GROUPS, 2):
        kept.append(jnp.where(yy == 0, lowrank[16 * c : 16 * c + 16], lowrank[16 * c + 16 : 16 * c + 32]))
    kept = jnp.concatenate(kept, 0).astype(BF16)
    lowrank = lowrank.astype(BF16)

    def adapter_term(rows, k):
        cols = pl.ds(pl.multiple_of(k * CHUNK, CHUNK), CHUNK)
        return jnp.dot(rows, vbuf[:, cols], preferred_element_type=F32)


    def z_copy(k, d):
        z_to = lax.rem(zz + d, 4)
        return remote(
            zstage.at[k, z_to], zrecv.at[k, zz], zs_sem.at[k, z_to], zr_sem.at[k, zz], z_to * 4 + lax.rem(me, 4)
        )

    def z_arrival(k, d):
        z_from = lax.rem(zz + d, 4)
        return remote(
            zstage.at[k, zz], zrecv.at[k, z_from], zs_sem.at[k, z_from], zr_sem.at[k, z_from], z_from * 4 + lax.rem(me, 4)
        )

    def turn(k, early):
        y_copy(k).wait_recv()
        pair = yown[k] + yrecv[k].astype(F32)
        if early:
            v_move(k, spare).wait_recv()
            pair += adapter_term(kept, k).reshape(pair.shape)
        zstage[k] = pair.astype(BF16)
        yown[k] = pair
        for d in range(1, 4):
            z_copy(k, d).start()

    def f_copy(k):
        return remote(fin.at[k], frecv.at[k], fs_sem.at[k], fr_sem.at[k], sibling)

    def finish(k):
        for d in range(1, 4):
            z_arrival(k, d).wait_recv()
        value = yown[k, zz]
        for d in range(1, 4):
            value += zrecv[k, lax.rem(zz + d, 4)].astype(F32)
        fin[k] = value.astype(BF16)
        f_copy(k).start()

    @pl.loop(EARLY, HELD)
    def _(k):
        send_y(k, acc[k] + adapter_term(lowrank, k))

    @pl.loop(0, EARLY)
    def _(k):
        turn(k, True)

    @pl.loop(HELD, chunks)
    def _(k):
        send_y(k, product(k) + adapter_term(lowrank, k))

    @pl.loop(EARLY, chunks)
    def _(k):
        turn(k, False)
        finish(k - EARLY)

    @pl.loop(chunks - EARLY, chunks)
    def _(k):
        finish(k)

    def rows_of(value):
        value = value.astype(F32)
        rows = value.shape[0] // 2
        return jnp.where(side == 0, value[:rows], value[rows:]).astype(out.dtype)

    @pl.loop(0, chunks)
    def _(k):
        f_copy(k).wait_recv()
        left = pl.multiple_of(side * (chunks * CHUNK) + k * CHUNK, 128)
        right = pl.multiple_of((1 - side) * (chunks * CHUNK) + k * CHUNK, 128)
        out[:, pl.ds(left, CHUNK)] = rows_of(fin[k])
        out[:, pl.ds(right, CHUNK)] = rows_of(frecv[k])

    @pl.loop(1, n)
    def _(d):
        p_copy(d).wait_send()
        a_copy(d).wait_send()
        l_copy(d).wait_send()

    for k in range(EARLY):
        v_move(k, own_rank).wait_send()

    @pl.loop(0, chunks)
    def _(k):
        y_copy(k).wait_send()
        f_copy(k).wait_send()
        for d in range(1, 4):
            z_copy(k, d).wait_send()


def fused(hidden, adapter_ids, core_slot, down_weight, rank_in, rank_out, cores):
    n = lax.axis_size("wide")
    tokens, units = hidden.shape
    rows, width = down_weight.shape[1:]
    chunks = width // CHUNK
    rank = rank_in.shape[1]
    adapters = core_slot.shape[0]
    anywhere = pl.BlockSpec(memory_space=pl.ANY)
    local = pl.BlockSpec(memory_space=pltpu.VMEM)
    dma = pltpu.SemaphoreType.DMA
    return pl.pallas_call(
        kernel,
        out_shape=jax.ShapeDtypeStruct((tokens // n, 2 * width), BF16),
        in_specs=[local] * 2 + [anywhere] * 5,
        out_specs=local,
        scratch_shapes=[
            pltpu.VMEM((tokens, rows), BF16),
            pltpu.VMEM((chunks, rows, CHUNK), BF16),
            pltpu.VMEM(rank_in.shape, BF16),
            pltpu.VMEM(cores.shape, BF16),
            pltpu.VMEM((128, width), BF16),
            pltpu.VMEM((HELD, tokens, CHUNK), F32),
            pltpu.VMEM((n, 16, rank // 2), BF16),
            pltpu.VMEM((n, 16, rank // 2), BF16),
            pltpu.VMEM((n, 16, rank // 2), BF16),
            pltpu.VMEM((tokens, rank), BF16),
            pltpu.VMEM((rank // 128, OWNER_CAP, 128), BF16),
            pltpu.VMEM((n, OWNER_CAP, 128), BF16),
            pltpu.VMEM((chunks, 4, 16, CHUNK), BF16),
            pltpu.VMEM((chunks, 4, 16, CHUNK), F32),
            pltpu.VMEM((chunks, 4, 16, CHUNK), BF16),
            pltpu.VMEM((chunks, 4, 16, CHUNK), BF16),
            pltpu.VMEM((chunks, 4, 16, CHUNK), BF16),
            pltpu.VMEM((chunks, 16, CHUNK), BF16),
            pltpu.VMEM((chunks, 16, CHUNK), BF16),
            dma((4,)), dma((chunks,)), dma((2,)),
            dma((n,)), dma((n,)), dma((n,)), dma((n,)), dma((n,)), dma((n,)),
            dma((chunks,)), dma((chunks,)), dma((chunks, 4)), dma((chunks, 4)),
            dma((chunks,)), dma((chunks,)), dma((EARLY,)), dma((EARLY,)),
        ],
        compiler_params=pltpu.CompilerParams(
            collective_id=0, has_side_effects=True, vmem_limit_bytes=60 * 1024 * 1024
        ),
        cost_estimate=pl.CostEstimate(
            flops=2 * tokens * rows * width, bytes_accessed=2 * rows * width, transcendentals=0
        ),
    )(
        adapter_ids.reshape(1, tokens), core_slot.reshape(1, adapters),
        hidden, down_weight, rank_in, rank_out, cores,
    )


def fits(devices, args):
    hidden, down_weight, rank_in = args[0], args[3], args[4]
    return (
        devices == 2 * FF_GROUPS
        and hidden.shape[0] == 16 * FF_GROUPS
        and rank_in.shape[1] == 64 * FF_GROUPS
        and down_weight.shape[2] % CHUNK == 0
        and down_weight.shape[2] // CHUNK >= HELD
    )


def shards(*args):
    return fused(*args) if fits(lax.axis_size("wide"), args) else general(*args)


def solution(mesh):
    return jax.shard_map(
        shards,
        mesh=mesh,
        in_specs=(
            P("groups", "wide"),
            P("groups"),
            P("groups"),
            P("wide", None, None),
            P("wide", None),
            P("wide", None, None),
            P("wide", None, None),
        ),
        out_specs=P(("groups", "wide"), None),
        check_vma=False,
    )
```
